512 devices in a mesh: tok: 8 (over z), code: 64 (over x, y, core).
Axes of the slice: x: 4, y: 8, z: 8, core: 2. Of those that a mesh axis runs over, the one named last changes fastest.
Arguments:
- latents: bfloat16 [8192, 1024], P(('tok', 'code')), may hold values from -24 to 24
- w_down: bfloat16 [1024, 256], replicated, may hold values from -0.1875 to 0.1875
- w_up: bfloat16 [256, 1024], replicated, may hold values from -0.375 to 0.375
- codebook: bfloat16 [131072, 256], P('code'), may hold values from -24 to 24
- grad_out: bfloat16 [8192, 1024], P(('tok', 'code')), may hold values from -6 to 6
Outputs:
- quantized: bfloat16 [8192, 1024], P(('tok', 'code'))
- grad_latents: bfloat16 [8192, 1024], P(('tok', 'code'))
- grad_codebook: float32 [131072, 256], P(('code', 'tok'))
The draws below stay inside these ranges and needn't reach their ends.
All inputs are finite; a program needn't handle non-finite values.
Results may differ from the reference program's by a relative error of at most 0.018.
Values may be sent and summed in bfloat16 or wider, within the bound.
A program may use at most 64 MiB of HBM per device.

```python
import math
import jax
import jax.numpy as jnp
from jax import lax

D = 1024
LAT = 256
TOK_BLK = 1024
CODES = 131072
TOKENS = 8192
N_TOK = 8


def rough_scales(key, rows, cols, low, high, base):
    key_row, key_col = jax.random.split(key, 2)
    row_scale = jnp.exp(jax.random.uniform(key_row, (rows, 1), jnp.float32, math.log(low), math.log(high)))
    col_scale = jnp.exp(jax.random.uniform(key_col, (1, cols), jnp.float32, math.log(0.5), math.log(2.0)))
    return base * row_scale * col_scale


def draw_latents(key, part):
    key = jax.random.fold_in(key, 11)
    key_base = jax.random.fold_in(key, 0)
    key_scale = jax.random.fold_in(key, 2)
    base = jnp.clip(jax.random.normal(key_base, (TOKENS, D), jnp.float32), -4.0, 4.0)
    return rough_scales(key_scale, TOKENS, D, 0.3, 3.0, base).astype(jnp.bfloat16)


def draw_codebook(key, part):
    key = jax.random.fold_in(key, 23)
    key_base = jax.random.fold_in(key, 0)
    key_scale = jax.random.fold_in(key, 2)
    base = jnp.clip(jax.random.normal(key_base, (CODES, LAT), jnp.float32), -4.0, 4.0)
    return rough_scales(key_scale, CODES, LAT, 0.3, 3.0, base).astype(jnp.bfloat16)


def shard_levels(key, shape, cuts, least, top_value):
    def one(dim, blocks):
        draws = jax.random.uniform(jax.random.fold_in(jax.random.fold_in(key, 6), dim), (blocks,), jnp.float32, least / len(cuts), top_value / len(cuts))
        return jnp.repeat(jnp.exp(draws), shape[dim] // blocks).reshape((-1,) + (1,) * (len(shape) - dim - 1))

    gain = one(*cuts[0])
    for cut in cuts[1:]:
        gain = gain * one(*cut)
    return gain


def scatter_about(own_key, dims, spread, limit, cuts=(), kind=jnp.bfloat16):
    factor_of = shard_levels(own_key, dims, cuts, -0.22, 0.18) if cuts else 1.0
    entries = jax.random.normal(own_key, dims, jnp.float32) * spread * factor_of
    return jnp.minimum(jnp.maximum(entries, -limit), limit).astype(kind)


def setup_inputs(seed: int = 0) -> dict:
    splits = jax.random.split(jax.random.key(seed), 6)
    return {
        "latents": draw_latents(jax.random.fold_in(splits[5], 71), 0),
        "w_down": scatter_about(splits[1], (D, LAT), D ** -0.5, 0.1875),
        "w_up": scatter_about(splits[2], (LAT, D), LAT ** -0.5, 0.375),
        "codebook": draw_codebook(jax.random.fold_in(splits[5], 71), 0),
        "grad_out": scatter_about(splits[4], (TOKENS, D), 1.0, 6.0, ((0, 512),)),
    }


logit_scale = 64.0
epsilon = 1e-06

def reference(latents, w_down, w_up, codebook, grad_out):
    code_f = codebook.astype(jnp.float32)
    cnorm = jnp.sqrt(lax.optimization_barrier(jnp.sum(code_f * code_f, axis=1, keepdims=True)) + epsilon)
    normed = code_f / cnorm
    normalized_lower = normed.astype(jnp.bfloat16)
    projected = jnp.dot(latents, w_down, preferred_element_type=jnp.float32)
    lnorm = jnp.sqrt(lax.optimization_barrier(jnp.sum(projected * projected, axis=1, keepdims=True)) + epsilon)
    unit = projected / lnorm
    unit_code_lower = unit.astype(jnp.bfloat16)
    grad_soft = jnp.dot(grad_out, w_up.T, preferred_element_type=jnp.float32)

    def block_step(total, pieces):
        unit_code_block, gsoft_blk = pieces
        logits = logit_scale * jnp.dot(unit_code_block, normalized_lower.T, preferred_element_type=jnp.float32)
        expo = jnp.exp(logits)
        denom = lax.optimization_barrier(jnp.sum(expo, axis=1))
        weights = expo.astype(jnp.bfloat16)
        soft = jnp.dot(weights, normalized_lower, preferred_element_type=jnp.float32) / denom[:, None]
        inner = lax.optimization_barrier(jnp.sum(gsoft_blk * soft, axis=1))
        grad_low = gsoft_blk.astype(jnp.bfloat16)
        prob = expo / denom[:, None]
        hits = jnp.dot(grad_low, normalized_lower.T, preferred_element_type=jnp.float32)
        logit_gradient = logit_scale * prob * (hits - inner[:, None])
        logit_gradient_lower = logit_gradient.astype(jnp.bfloat16)
        prob_low = prob.astype(jnp.bfloat16)
        gradient_term = jnp.dot(prob_low.T, grad_low, preferred_element_type=jnp.float32)
        gradient_term = gradient_term + jnp.dot(logit_gradient_lower.T, unit_code_block, preferred_element_type=jnp.float32)
        rounded = lax.optimization_barrier(gradient_term.astype(jnp.bfloat16))
        total = total + rounded.astype(jnp.float32)
        unit_code_gradient = jnp.dot(logit_gradient_lower, normalized_lower, preferred_element_type=jnp.float32)
        return (total, (soft, unit_code_gradient))
    start_total = jnp.zeros((CODES, LAT), jnp.float32)
    grad_normed, outs = lax.scan(block_step, start_total, (unit_code_lower.reshape(N_TOK, TOK_BLK, LAT), grad_soft.reshape(N_TOK, TOK_BLK, LAT)))
    soft = outs[0].reshape(TOKENS, LAT)
    unit_code_gradient = outs[1].reshape(TOKENS, LAT)
    quantized = jnp.dot(soft.astype(jnp.bfloat16), w_up, preferred_element_type=jnp.float32).astype(jnp.bfloat16)
    grad_codebook = (grad_normed - normed * lax.optimization_barrier(jnp.sum(normed * grad_normed, axis=1, keepdims=True))) / cnorm
    grad_proj = ((unit_code_gradient - unit * lax.optimization_barrier(jnp.sum(unit * unit_code_gradient, axis=1, keepdims=True))) / lnorm).astype(jnp.bfloat16)
    grad_latents = jnp.dot(grad_proj, w_down.T, preferred_element_type=jnp.float32).astype(jnp.bfloat16)
    return (quantized, grad_latents, grad_codebook)
```

```python
import functools

import jax
import jax.numpy as jnp
from jax import lax
from jax.experimental import pallas as pl
from jax.experimental.pallas import tpu as pltpu
from jax.sharding import PartitionSpec as P

MESH = pl.DeviceIdType.MESH
F32 = jnp.float32
BF16 = jnp.bfloat16

logit_scale = 64.0
epsilon = 1e-06
X_CHIPS = 4
CORES = 2


def dot_nn(a, b):
    return lax.dot_general(a, b, (((1,), (0,)), ((), ())), preferred_element_type=F32)


def dot_nt(a, b):
    return lax.dot_general(a, b, (((1,), (1,)), ((), ())), preferred_element_type=F32)


def longest(n, sign, half):
    return n // 2 if (sign > 0) == (half == 0) else n // 2 - 1


class RingSum:
    def __init__(self, n, out, into, send_sem, recv_sem, peer):
        self.n, self.out, self.into = n, out, into
        self.send_sem, self.recv_sem, self.peer = send_sem, recv_sem, peer
        self.sent = []

    def copy(self, sign, k, half):
        at = (0 if sign > 0 else 1, k - 1, half)
        return pltpu.make_async_remote_copy(
            src_ref=self.out.at[at],
            dst_ref=self.into.at[at],
            send_sem=self.send_sem.at[at],
            recv_sem=self.recv_sem.at[at],
            device_id=self.peer(sign),
            device_id_type=MESH,
        )

    def arrived(self, sign, k, half):
        self.copy(sign, k, half).wait_recv()
        return self.into[0 if sign > 0 else 1, k - 1, half].astype(F32)

    def send(self, sign, k, half, term):
        top = longest(self.n, sign, half)
        if k > top:
            return
        if k < top:
            term = term + self.arrived(sign, k + 1, half)
        self.out[0 if sign > 0 else 1, k - 1, half] = term.astype(BF16)
        copy = self.copy(sign, k, half)
        copy.start()
        self.sent.append(copy)

    def total(self, half, term):
        for sign in (1, -1):
            if longest(self.n, sign, half) >= 1:
                term = term + self.arrived(sign, 1, half)
        return term


def kernel(
    x_n, y_n, z_n,
    lat_h, wd_h, wu_h, cb_h, go_h,
    q_out, gl_out, gcb_out,
    lat, wd, wu, cb, go, load_sem,
    gat, low, low_t, ee, wt, tr, na, na_in, grad, own,
    ay_s, ay_r, ax_s, ax_r, ah_s, ah_r, as_s, as_r,
    st, st_c_in, st_y_in, st_x_in,
    sc_s, sc_r, sy_s, sy_r, sx_s, sx_r,
    nc_s, nc_r, xo, xi, xo_s, xo_r,
    yo, yi, yo_s, yo_r, fo, fi, fo_s, fo_r,
    zo, zi, zo_s, zo_r,
):
    tok = lax.axis_index("tok")
    code = lax.axis_index("code")
    core = lax.rem(code, CORES)
    y = lax.rem(code // CORES, y_n)
    x = code // (CORES * y_n)
    rows = lat_h.shape[0]
    lat_w = wd_h.shape[1]
    codes = cb_h.shape[0]
    block = y_n * rows
    width = CORES * block
    half_codes = codes // z_n // 2
    half_lat = lat_w // 2

    def at_code(x_at, y_at, core_at):
        return {"code": (x_at * y_n + y_at) * CORES + core_at}

    sibling = at_code(x, y, 1 - core)

    def y_peer(step):
        return at_code(x, lax.rem(y + step, y_n), core)

    def x_peer(step):
        return at_code(lax.rem(x + step + x_n, x_n), y, core)

    def z_peer(step):
        return {"tok": lax.rem(tok + step + z_n, z_n)}

    def remote(src, dst, send_sem, recv_sem, device):
        return pltpu.make_async_remote_copy(
            src_ref=src, dst_ref=dst, send_sem=send_sem, recv_sem=recv_sem, device_id=device, device_id_type=MESH
        )

    sent = []

    def push(*args):
        copy = remote(*args)
        copy.start()
        sent.append(copy)

    def pull(dst, recv_sem, device):
        remote(dst, dst, as_s.at[0], recv_sem, device).wait_recv()

    loads = [
        pltpu.make_async_copy(src, dst, load_sem.at[i])
        for i, (src, dst) in enumerate(((lat_h, lat), (wd_h, wd), (go_h, go), (wu_h, wu), (cb_h, cb)))
    ]
    for load in loads:
        load.start()

    peers = [sibling] + [y_peer(s) for s in range(1, y_n)] + [x_peer(s) for s in range(1, x_n)]
    peers += [z_peer(1), z_peer(-1)]
    barrier = pltpu.get_barrier_semaphore()
    for peer in peers:
        pl.semaphore_signal(barrier, inc=1, device_id=peer, device_id_type=MESH)

    loads[0].wait()
    loads[1].wait()
    proj = dot_nn(lat[...], wd[...])
    lnorm = jnp.sqrt(jnp.sum(proj * proj, axis=1, keepdims=True) + epsilon)
    unit = proj / lnorm
    own[0] = unit
    own[1] = jnp.broadcast_to(lnorm, unit.shape)
    own_rows = pl.ds(pl.multiple_of(core * block + y * rows, rows), rows)
    gat[0, 0, own_rows, :] = (unit.astype(BF16).astype(F32) * logit_scale).astype(BF16)
    loads[2].wait()
    loads[3].wait()
    gat[0, 1, own_rows, :] = dot_nt(go[...], wu[...]).astype(BF16)

    pl.semaphore_wait(barrier, len(peers))

    for s in range(1, y_n):
        piece = gat.at[0, :, own_rows, :]
        push(piece, piece, ay_s.at[s - 1], ay_r.at[s - 1], y_peer(s))

    loads[4].wait()
    step_rows = min(256, codes)

    def normalize(i, _):
        at = pl.ds(pl.multiple_of(i * step_rows, step_rows), step_rows)
        c = cb[at, :].astype(F32)
        n = c / jnp.sqrt(jnp.sum(c * c, axis=1, keepdims=True) + epsilon)
        n = n.astype(BF16)
        low[at, :] = n
        low_t[:, at] = n.T
        return 0

    lax.fori_loop(0, codes // step_rows, normalize, 0)

    my_block = pl.ds(pl.multiple_of(core * block, block), block)
    its_block = pl.ds(pl.multiple_of((1 - core) * block, block), block)
    first_half = pl.ds(pl.multiple_of(core * block, block // 2), block // 2)
    second_half = pl.ds(pl.multiple_of(core * block + block // 2, block // 2), block // 2)

    for s in range(1, y_n):
        from_y = lax.rem(y + y_n - s, y_n)
        at = pl.ds(pl.multiple_of(core * block + from_y * rows, rows), rows)
        pull(gat.at[0, :, at, :], ay_r.at[s - 1], y_peer(s))

    def to_sibling(j):
        piece = gat.at[j, :, my_block, :]
        push(piece, piece, as_s.at[j], as_r.at[j], sibling)

    def from_sibling(j):
        pull(gat.at[j, :, its_block, :], as_r.at[j], sibling)

    mine = gat.at[0, :, my_block, :]
    push(mine, gat.at[x_n - 1, :, my_block, :], ax_s.at[0], ax_r.at[0], x_peer(1))
    push(mine, gat.at[1, :, my_block, :], ax_s.at[1], ax_r.at[1], x_peer(-1))
    to_sibling(0)

    tile = min(512, codes)
    sums = {}

    def forward(j):
        u = gat[j, 0]
        g = gat[j, 1]
        col = pl.ds(j * width, width)
        col_h = pl.ds((x_n + j) * width, width)

        def step(i, carry):
            den, inn = carry
            at = pl.ds(pl.multiple_of(i * tile, tile), tile)
            n = low[at, :]
            e = jnp.exp(dot_nt(n, u))
            eh = e * dot_nt(n, g)
            ee[at, col] = e.astype(BF16)
            ee[at, col_h] = eh.astype(BF16)
            return den + e.reshape(tile // 8, 8, width).sum(0), inn + eh.reshape(tile // 8, 8, width).sum(0)

        zero = jnp.zeros((8, width), F32)
        den, inn = lax.fori_loop(0, codes // tile, step, (zero, zero))
        sums[j] = (jnp.sum(den, axis=0, keepdims=True), jnp.sum(inn, axis=0, keepdims=True))
        tr[j, 0] = u.T
        tr[j, 1] = g.T

    def weighted(j):
        na[j, 0] = dot_nn(low_t[...], ee[:, pl.ds(j * width, width)]).astype(BF16)
        na[j, 1] = dot_nn(low_t[...], ee[:, pl.ds((x_n + j) * width, width)]).astype(BF16)
        push(na.at[j, 1 - core], na_in.at[j], nc_s.at[j], nc_r.at[j], sibling)

    from_sibling(0)
    forward(0)

    pull(gat.at[x_n - 1, :, my_block, :], ax_r.at[0], x_peer(-1))
    push(
        gat.at[x_n - 1, :, first_half, :], gat.at[2, :, first_half, :], ah_s.at[0], ah_r.at[0], x_peer(1)
    )
    to_sibling(x_n - 1)
    pull(gat.at[1, :, my_block, :], ax_r.at[1], x_peer(1))
    push(gat.at[1, :, second_half, :], gat.at[2, :, second_half, :], ah_s.at[1], ah_r.at[1], x_peer(-1))
    to_sibling(1)

    weighted(0)
    from_sibling(x_n - 1)
    forward(x_n - 1)
    from_sibling(1)
    forward(1)
    pull(gat.at[2, :, first_half, :], ah_r.at[0], x_peer(-1))
    pull(gat.at[2, :, second_half, :], ah_r.at[1], x_peer(1))
    to_sibling(2)
    weighted(x_n - 1)
    weighted(1)
    from_sibling(2)
    forward(2)

    line = lax.broadcasted_iota(jnp.int32, (2 * x_n, width), 0)
    part = jnp.zeros((2 * x_n, width), F32)
    for j in range(x_n):
        at_x = lax.rem(x + j, x_n)
        part = jnp.where(line == 2 * at_x, sums[j][0], part)
        part = jnp.where(line == 2 * at_x + 1, sums[j][1], part)
    st[0] = part
    push(st.at[0], st_c_in, sc_s.at[0], sc_r.at[0], sibling)
    weighted(2)
    pull(st_c_in, sc_r.at[0], sibling)
    st[1] = part = part + st_c_in[...]
    for s in range(1, y_n):
        push(st.at[1], st_y_in.at[s - 1], sy_s.at[s - 1], sy_r.at[s - 1], y_peer(s))

    ring_x = RingSum(x_n, xo, xi, xo_s, xo_r, x_peer)

    def paired(j, half):
        at = pl.ds(half * half_lat, half_lat)
        return na[j, core, at, :].astype(F32) + na_in[j, at, :].astype(F32)

    for j in range(x_n):
        pull(na_in.at[j], nc_r.at[j], sibling)

    for s in range(1, y_n):
        pull(st_y_in.at[s - 1], sy_r.at[s - 1], y_peer(s))
        part = part + st_y_in[s - 1]
    st[2] = part
    for s in range(1, x_n):
        push(st.at[2], st_x_in.at[s - 1], sx_s.at[s - 1], sx_r.at[s - 1], x_peer(s))
    for s in range(1, x_n):
        pull(st_x_in.at[s - 1], sx_r.at[s - 1], x_peer(s))
    total = jnp.zeros((2 * x_n, width), F32)
    for at_x in range(x_n):
        term = jnp.where(x == at_x, part, 0.0)
        for s in range(1, x_n):
            term = jnp.where(lax.rem(x + x_n - s, x_n) == at_x, st_x_in[s - 1], term)
        total = total + term

    def line_of(at):
        return jnp.sum(jnp.where(line == at, total, 0.0), axis=0, keepdims=True)

    for j in range(x_n):
        at_x = lax.rem(x + j, x_n)
        den = line_of(2 * at_x)
        inner = line_of(2 * at_x + 1) / den
        inv = 1.0 / den
        ut = tr[j, 0].astype(F32)
        gt = tr[j, 1].astype(F32)
        wt[:, pl.ds(j * width, width)] = ((gt - inner * ut) * inv).astype(BF16)
        wt[:, pl.ds((x_n + j) * width, width)] = (ut * inv).astype(BF16)

    ring_z = RingSum(z_n, zo, zi, zo_s, zo_r, z_peer)
    share = codes // z_n

    def shard(step):
        at = pl.ds(pl.multiple_of(lax.rem(tok + step + z_n, z_n) * share, share), share)
        grad[step % z_n] = dot_nt(ee[at, :], wt[...])

    def send_z(sign, k, half):
        ring_z.send(sign, k, half, grad[(sign * k) % z_n, pl.ds(half * half_codes, half_codes), :])

    def send_x(sign, k, half):
        ring_x.send(sign, k, half, paired((sign * k) % x_n, half))

    top = z_n // 2
    shard(top)
    send_z(1, top, 0)
    send_z(-1, top, 1)
    send_x(1, 2, 0)
    send_x(-1, 2, 1)
    send_x(1, 1, 1)
    send_x(-1, 1, 0)

    done = {top}

    def shards(k):
        if k < 1:
            return
        for sign in (1, -1):
            if (sign * k) % z_n not in done:
                shard(sign * k)
                done.add((sign * k) % z_n)

    def late_x():
        send_x(1, 1, 0)
        send_x(-1, 1, 1)

    def tokens_y():
        for half in range(2):
            both = ring_x.total(half, paired(0, half)).T.astype(BF16)
            for to_core in range(CORES):
                for to_y in range(y_n):
                    first = to_core * block + to_y * rows
                    yo[to_y, to_core * rows : (to_core + 1) * rows, half * half_lat : (half + 1) * half_lat] = both[
                        first : first + rows
                    ]
        for s in range(1, y_n):
            push(yo.at[lax.rem(y + s, y_n)], yi.at[s - 1], yo_s.at[s - 1], yo_r.at[s - 1], y_peer(s))

    def tokens_core():
        chip = yo[y].astype(F32)
        for s in range(1, y_n):
            pull(yi.at[s - 1], yo_r.at[s - 1], y_peer(s))
            chip = chip + yi[s - 1].astype(F32)
        fo[0] = chip[:rows]
        fo[1] = chip[rows:]
        push(fo.at[1 - core], fi, fo_s.at[0], fo_r.at[0], sibling)

    between = {top - 1: late_x, top - 2: tokens_y, top - 3: tokens_core}
    for k in range(top - 1, 0, -1):
        shards(k)
        if k == top - 1:
            send_z(1, k, 1)
            send_z(-1, k, 0)
            shards(k - 1)
            send_z(1, k, 0)
            send_z(-1, k, 1)
        else:
            send_z(1, k, 1)
            send_z(-1, k, 0)
            send_z(1, k, 0)
            send_z(-1, k, 1)
        if k in between:
            between.pop(k)()
    shard(0)
    for k in sorted(between, reverse=True):
        between[k]()

    pull(fi, fo_r.at[0], sibling)
    kept, given = fo[core], fi[...]
    numer = jnp.where(core == 0, kept, given)
    pulled = jnp.where(core == 0, given, kept)
    lane = lax.broadcasted_iota(jnp.int32, (rows, width), 1)
    first = lax.broadcasted_iota(jnp.int32, (rows, width), 0) + (core * block + y * rows)

    def column(at):
        return jnp.sum(jnp.where(lane == first, line_of(at), 0.0), axis=1, keepdims=True)

    den = column(2 * x)
    inner = column(2 * x + 1) / den
    soft = numer / den
    q_out[...] = dot_nn(soft.astype(BF16), wu[...]).astype(BF16)
    grad_unit = (pulled - inner * numer) / den * logit_scale
    unit = own[0]
    grad_proj = (grad_unit - unit * jnp.sum(unit * grad_unit, axis=1, keepdims=True)) / own[1]
    gl_out[...] = dot_nt(grad_proj.astype(BF16), wd[...]).astype(BF16)

    for half in range(2):
        at = pl.ds(half * half_codes, half_codes)
        c = cb[pl.ds(pl.multiple_of(tok * share + half * half_codes, half_codes), half_codes), :].astype(F32)
        cnorm = jnp.sqrt(jnp.sum(c * c, axis=1, keepdims=True) + epsilon)
        n = c / cnorm
        gn = ring_z.total(half, grad[0, at, :])
        gcb_out[at, :] = (gn - n * jnp.sum(n * gn, axis=1, keepdims=True)) / cnorm

    for copy in sent + ring_x.sent + ring_z.sent:
        copy.wait_send()


def solution(mesh):
    z_n = mesh.shape["tok"]
    x_n = X_CHIPS
    y_n = mesh.shape["code"] // (CORES * x_n)

    def local(latents, w_down, w_up, codebook, grad_out):
        rows, d = latents.shape
        lat_w = w_down.shape[1]
        codes = codebook.shape[0]
        width = CORES * y_n * rows
        sem = lambda *shape: pltpu.SemaphoreType.DMA(shape)
        ring = lambda n, r, w: [
            pltpu.VMEM((2, n // 2, 2, r, w), BF16),
            pltpu.VMEM((2, n // 2, 2, r, w), BF16),
            sem(2, n // 2, 2),
            sem(2, n // 2, 2),
        ]
        any_space = pl.BlockSpec(memory_space=pl.ANY)
        vmem = pl.BlockSpec(memory_space=pltpu.VMEM)
        stats = (2 * x_n, width)
        return pl.pallas_call(
            functools.partial(kernel, x_n, y_n, z_n),
            out_shape=(
                jax.ShapeDtypeStruct((rows, d), BF16),
                jax.ShapeDtypeStruct((rows, d), BF16),
                jax.ShapeDtypeStruct((codes // z_n, lat_w), F32),
            ),
            in_specs=[any_space] * 5,
            out_specs=(vmem, vmem, vmem),
            scratch_shapes=[
                pltpu.VMEM(latents.shape, BF16),
                pltpu.VMEM(w_down.shape, BF16),
                pltpu.VMEM(w_up.shape, BF16),
                pltpu.VMEM(codebook.shape, BF16),
                pltpu.VMEM(grad_out.shape, BF16),
                sem(5),
                pltpu.VMEM((x_n, 2, width, lat_w), BF16),
                pltpu.VMEM((codes, lat_w), BF16),
                pltpu.VMEM((lat_w, codes), BF16),
                pltpu.VMEM((codes, 2 * x_n * width), BF16),
                pltpu.VMEM((lat_w, 2 * x_n * width), BF16),
                pltpu.VMEM((x_n, 2, lat_w, width), BF16),
                pltpu.VMEM((x_n, 2, lat_w, width), BF16),
                pltpu.VMEM((x_n, lat_w, width), BF16),
                pltpu.VMEM((z_n, codes // z_n, lat_w), F32),
                pltpu.VMEM((2, rows, lat_w), F32),
                sem(y_n - 1), sem(y_n - 1), sem(2), sem(2), sem(2), sem(2), sem(x_n), sem(x_n),
                pltpu.VMEM((3,) + stats, F32),
                pltpu.VMEM(stats, F32),
                pltpu.VMEM((y_n - 1,) + stats, F32),
                pltpu.VMEM((x_n - 1,) + stats, F32),
                sem(1), sem(1), sem(y_n - 1), sem(y_n - 1), sem(x_n - 1), sem(x_n - 1),
                sem(x_n), sem(x_n),
                *ring(x_n, lat_w // 2, width),
                pltpu.VMEM((y_n, CORES * rows, lat_w), BF16),
                pltpu.VMEM((y_n - 1, CORES * rows, lat_w), BF16),
                sem(y_n - 1), sem(y_n - 1),
                pltpu.VMEM((CORES, rows, lat_w), F32),
                pltpu.VMEM((rows, lat_w), F32),
                sem(1), sem(1),
                *ring(z_n, codes // z_n // 2, lat_w),
            ],
            compiler_params=pltpu.CompilerParams(
                collective_id=0, has_side_effects=True, vmem_limit_bytes=52 * 2**20
            ),
        )(latents, w_down, w_up, codebook, grad_out)

    return jax.shard_map(
        local,
        mesh=mesh,
        in_specs=(P(("tok", "code"), None), P(), P(), P("code", None), P(("tok", "code"), None)),
        out_specs=(P(("tok", "code"), None), P(("tok", "code"), None), P(("code", "tok"), None)),
        check_vma=False,
    )
```

```python
import functools
import itertools

import jax
import jax.numpy as jnp
from jax import lax
from jax.experimental import pallas as pl
from jax.experimental.pallas import tpu as pltpu
from jax.sharding import PartitionSpec as P

MESH = pl.DeviceIdType.MESH
F32 = jnp.float32
BF16 = jnp.bfloat16

logit_scale = 64.0
epsilon = 1e-06
X_CHIPS = 4
CORES = 2


def dot_nn(a, b):
    return lax.dot_general(a, b, (((1,), (0,)), ((), ())), preferred_element_type=F32)


def dot_nt(a, b):
    return lax.dot_general(a, b, (((1,), (1,)), ((), ())), preferred_element_type=F32)


def longest(n, parts, sign, part):
    return n // 2 if (sign > 0) == (part < parts // 2) else n // 2 - 1


class RingSum:
    def __init__(self, n, out, into, send_sem, recv_sem, peer):
        self.n, self.out, self.into = n, out, into
        self.parts = out.shape[2]
        self.send_sem, self.recv_sem, self.peer = send_sem, recv_sem, peer
        self.sent = []

    def order(self, sign):
        listed = []
        for k in range(self.n // 2, 0, -1):
            parts = sorted(range(self.parts), key=lambda p: (longest(self.n, self.parts, sign, p), p))
            listed += [(k, p) for p in parts if k <= longest(self.n, self.parts, sign, p)]
        return listed

    def copy(self, sign, k, part):
        at = (0 if sign > 0 else 1, k - 1, part)
        return pltpu.make_async_remote_copy(
            src_ref=self.out.at[at],
            dst_ref=self.into.at[at],
            send_sem=self.send_sem.at[at],
            recv_sem=self.recv_sem.at[at],
            device_id=self.peer(sign),
            device_id_type=MESH,
        )

    def arrived(self, sign, k, part):
        self.copy(sign, k, part).wait_recv()
        return self.into[0 if sign > 0 else 1, k - 1, part].astype(F32)

    def send(self, sign, k, part, term):
        if k < longest(self.n, self.parts, sign, part):
            term = term + self.arrived(sign, k + 1, part)
        self.out[0 if sign > 0 else 1, k - 1, part] = term.astype(BF16)
        copy = self.copy(sign, k, part)
        copy.start()
        self.sent.append(copy)

    def total(self, part, term):
        for sign in (1, -1):
            if longest(self.n, self.parts, sign, part) >= 1:
                term = term + self.arrived(sign, 1, part)
        return term


def kernel(
    x_n, y_n, z_n,
    lat_h, wd_h, wu_h, cb_h, go_h,
    q_out, gl_out, gcb_out,
    lat, wd, wu, cb, go, load_sem,
    gat, low, low_t, ee, wt, tr, na, na_in, grad, own,
    ay_s, ay_r, ax_s, ax_r, as_s, as_r,
    st, st_c_in, st_y_in, st_x_in,
    sc_s, sc_r, sy_s, sy_r, sx_s, sx_r,
    nc_s, nc_r, xo, xi, xo_s, xo_r,
    yo, yi, yo_s, yo_r, fo, fi, fo_s, fo_r,
    zo, zi, zo_s, zo_r,
):
    tok = lax.axis_index("tok")
    code = lax.axis_index("code")
    core = lax.rem(code, CORES)
    y = lax.rem(code // CORES, y_n)
    x = code // (CORES * y_n)
    rows = lat_h.shape[0]
    lat_w = wd_h.shape[1]
    codes = cb_h.shape[0]
    block = y_n * rows
    width = CORES * block
    z_parts = zo.shape[2]
    x_parts = xo.shape[2]
    z_rows = codes // z_n // z_parts
    x_rows = lat_w // x_parts

    def at_code(x_at, y_at, core_at):
        return {"code": (x_at * y_n + y_at) * CORES + core_at}

    sibling = at_code(x, y, 1 - core)

    def y_peer(step):
        return at_code(x, lax.rem(y + step, y_n), core)

    def x_peer(step):
        return at_code(lax.rem(x + step + x_n, x_n), y, core)

    def z_peer(step):
        return {"tok": lax.rem(tok + step + z_n, z_n)}

    def remote(src, dst, send_sem, recv_sem, device):
        return pltpu.make_async_remote_copy(
            src_ref=src, dst_ref=dst, send_sem=send_sem, recv_sem=recv_sem, device_id=device, device_id_type=MESH
        )

    sent = []

    def push(*args):
        copy = remote(*args)
        copy.start()
        sent.append(copy)

    def pull(dst, recv_sem, device):
        remote(dst, dst, as_s.at[0], recv_sem, device).wait_recv()

    loads = [
        pltpu.make_async_copy(src, dst, load_sem.at[i])
        for i, (src, dst) in enumerate(((lat_h, lat), (wd_h, wd), (go_h, go), (wu_h, wu), (cb_h, cb)))
    ]
    for load in loads:
        load.start()

    peers = [sibling] + [y_peer(s) for s in range(1, y_n)] + [x_peer(s) for s in range(1, x_n)]
    peers += [z_peer(1), z_peer(-1)]
    barrier = pltpu.get_barrier_semaphore()
    for peer in peers:
        pl.semaphore_signal(barrier, inc=1, device_id=peer, device_id_type=MESH)

    loads[0].wait()
    loads[1].wait()
    proj = dot_nn(lat[...], wd[...])
    lnorm = jnp.sqrt(jnp.sum(proj * proj, axis=1, keepdims=True) + epsilon)
    unit = proj / lnorm
    own[0] = unit
    own[1] = jnp.broadcast_to(lnorm, unit.shape)
    own_rows = pl.ds(pl.multiple_of(core * block + y * rows, rows), rows)
    gat[0, 0, own_rows, :] = (unit.astype(BF16).astype(F32) * logit_scale).astype(BF16)
    loads[2].wait()
    loads[3].wait()
    gat[0, 1, own_rows, :] = dot_nt(go[...], wu[...]).astype(BF16)

    pl.semaphore_wait(barrier, len(peers))

    near = sorted(range(1, y_n), key=lambda s: min(s, y_n - s))

    def along_x(s):
        from_y = lax.rem(y + y_n - s, y_n)
        at = pl.ds(pl.multiple_of(core * block + from_y * rows, rows), rows)
        for i, step in enumerate((2, 1, -1)):
            slot = -step % x_n
            push(gat.at[0, :, at, :], gat.at[slot, :, at, :], ax_s.at[s, i], ax_r.at[slot - 1], x_peer(step))

    for s in reversed(near):
        piece = gat.at[0, :, own_rows, :]
        push(piece, piece, ay_s.at[s - 1], ay_r.at[s - 1], y_peer(s))
    along_x(0)

    step_rows = min(256, codes)
    steps = codes // step_rows

    def normalize(i):
        at = pl.ds(i * step_rows, step_rows)
        c = cb[at, :].astype(F32)
        n = c / jnp.sqrt(jnp.sum(c * c, axis=1, keepdims=True) + epsilon)
        n = n.astype(BF16)
        low[at, :] = n
        low_t[:, at] = n.T

    loads[4].wait()
    ready = 0
    while ready < steps // 2:
        normalize(ready)
        ready += 1

    my_block = pl.ds(pl.multiple_of(core * block, block), block)
    its_block = pl.ds(pl.multiple_of((1 - core) * block, block), block)

    for s in near:
        from_y = lax.rem(y + y_n - s, y_n)
        at = pl.ds(pl.multiple_of(core * block + from_y * rows, rows), rows)
        pull(gat.at[0, :, at, :], ay_r.at[s - 1], y_peer(s))
        along_x(s)
        if ready < steps:
            normalize(ready)
            ready += 1
    while ready < steps:
        normalize(ready)
        ready += 1

    def to_sibling(j):
        piece = gat.at[j, :, my_block, :]
        push(piece, piece, as_s.at[j], as_r.at[j], sibling)

    def from_sibling(j):
        pull(gat.at[j, :, its_block, :], as_r.at[j], sibling)

    to_sibling(0)

    tile = min(512, codes)
    sums = {}

    def forward(j):
        u = gat[j, 0]
        g = gat[j, 1]
        col = pl.ds(j * width, width)
        col_h = pl.ds((x_n + j) * width, width)

        def step(i, carry):
            den, inn = carry
            at = pl.ds(pl.multiple_of(i * tile, tile), tile)
            n = low[at, :]
            e = jnp.exp(dot_nt(n, u))
            eh = e * dot_nt(n, g)
            ee[at, col] = e.astype(BF16)
            ee[at, col_h] = eh.astype(BF16)
            return den + e.reshape(tile // 8, 8, width).sum(0), inn + eh.reshape(tile // 8, 8, width).sum(0)

        zero = jnp.zeros((8, width), F32)
        den, inn = lax.fori_loop(0, codes // tile, step, (zero, zero), unroll=True)
        sums[j] = (jnp.sum(den, axis=0, keepdims=True), jnp.sum(inn, axis=0, keepdims=True))
        tr[j, 0] = u.T
        tr[j, 1] = g.T

    def weighted(j):
        na[j, 0] = dot_nn(low_t[...], ee[:, pl.ds(j * width, width)]).astype(BF16)
        na[j, 1] = dot_nn(low_t[...], ee[:, pl.ds((x_n + j) * width, width)]).astype(BF16)
        push(na.at[j, 1 - core], na_in.at[j], nc_s.at[j], nc_r.at[j], sibling)

    def from_x(j):
        pull(gat.at[j, :, my_block, :], ax_r.at[j - 1], x_peer(j))
        to_sibling(j)

    from_sibling(0)
    forward(0)
    from_x(x_n - 1)
    from_x(1)
    weighted(0)
    from_sibling(x_n - 1)
    forward(x_n - 1)
    from_x(2)
    from_sibling(1)
    forward(1)
    weighted(x_n - 1)
    from_sibling(2)
    forward(2)

    line = lax.broadcasted_iota(jnp.int32, (2 * x_n, width), 0)
    part = jnp.zeros((2 * x_n, width), F32)
    for j in range(x_n):
        at_x = lax.rem(x + j, x_n)
        part = jnp.where(line == 2 * at_x, sums[j][0], part)
        part = jnp.where(line == 2 * at_x + 1, sums[j][1], part)
    st[0] = part
    push(st.at[0], st_c_in, sc_s.at[0], sc_r.at[0], sibling)
    weighted(1)
    weighted(2)
    pull(st_c_in, sc_r.at[0], sibling)
    st[1] = part = part + st_c_in[...]
    for s in reversed(near):
        push(st.at[1], st_y_in.at[s - 1], sy_s.at[s - 1], sy_r.at[s - 1], y_peer(s))

    ring_x = RingSum(x_n, xo, xi, xo_s, xo_r, x_peer)

    def paired(j, part):
        at = pl.ds(part * x_rows, x_rows)
        return na[j, core, at, :].astype(F32) + na_in[j, at, :].astype(F32)

    def send_x(wanted):
        for sign in (1, -1):
            for k, part in ring_x.order(sign):
                if wanted(k == longest(x_n, x_parts, sign, part)):
                    ring_x.send(sign, k, part, paired((sign * k) % x_n, part))

    for j in range(x_n):
        pull(na_in.at[j], nc_r.at[j], sibling)
    send_x(lambda begins: begins)

    for s in range(1, y_n):
        pull(st_y_in.at[s - 1], sy_r.at[s - 1], y_peer(s))
        part = part + st_y_in[s - 1]
    st[2] = part
    for s in range(1, x_n):
        push(st.at[2], st_x_in.at[s - 1], sx_s.at[s - 1], sx_r.at[s - 1], x_peer(s))
    send_x(lambda begins: not begins)
    for s in range(1, x_n):
        pull(st_x_in.at[s - 1], sx_r.at[s - 1], x_peer(s))
    total = jnp.zeros((2 * x_n, width), F32)
    for at_x in range(x_n):
        term = jnp.where(x == at_x, part, 0.0)
        for s in range(1, x_n):
            term = jnp.where(lax.rem(x + x_n - s, x_n) == at_x, st_x_in[s - 1], term)
        total = total + term

    def line_of(at):
        return jnp.sum(jnp.where(line == at, total, 0.0), axis=0, keepdims=True)

    for j in range(x_n):
        at_x = lax.rem(x + j, x_n)
        den = line_of(2 * at_x)
        inner = line_of(2 * at_x + 1) / den
        inv = 1.0 / den
        ut = tr[j, 0].astype(F32)
        gt = tr[j, 1].astype(F32)
        wt[:, pl.ds(j * width, width)] = ((gt - inner * ut) * inv).astype(BF16)
        wt[:, pl.ds((x_n + j) * width, width)] = (ut * inv).astype(BF16)

    ring_z = RingSum(z_n, zo, zi, zo_s, zo_r, z_peer)
    share = codes // z_n

    def shard(step):
        at = pl.ds(pl.multiple_of(lax.rem(tok + step + z_n, z_n) * share, share), share)
        grad[step % z_n] = dot_nt(ee[at, :], wt[...])

    def send_z(sign, k, part):
        ring_z.send(sign, k, part, grad[(sign * k) % z_n, pl.ds(part * z_rows, z_rows), :])

    def tokens_y():
        for part in range(x_parts):
            both = ring_x.total(part, paired(0, part)).T.astype(BF16)
            for to_core in range(CORES):
                for to_y in range(y_n):
                    first = to_core * block + to_y * rows
                    yo[to_y, to_core * rows : (to_core + 1) * rows, part * x_rows : (part + 1) * x_rows] = both[
                        first : first + rows
                    ]
        for s in range(1, y_n):
            push(yo.at[lax.rem(y + s, y_n)], yi.at[s - 1], yo_s.at[s - 1], yo_r.at[s - 1], y_peer(s))

    def tokens_core():
        chip = yo[y].astype(F32)
        for s in range(1, y_n):
            pull(yi.at[s - 1], yo_r.at[s - 1], y_peer(s))
            chip = chip + yi[s - 1].astype(F32)
        fo[0] = chip[:rows]
        fo[1] = chip[rows:]
        push(fo.at[1 - core], fi, fo_s.at[0], fo_r.at[0], sibling)

    top = z_n // 2
    shard(top)
    computed = {top}
    after = {top: lambda: None, top - 1: tokens_y, top - 2: tokens_core}
    for k in range(top, 0, -1):
        messages = {sign: [m for m in ring_z.order(sign) if m[0] == k] for sign in (1, -1)}
        ahead = [(sign * k) % z_n for sign in (1, -1)]
        for step in ahead:
            if step not in computed:
                shard(step)
                computed.add(step)
        for pair in itertools.zip_longest(messages[1], messages[-1]):
            for sign, message in zip((1, -1), pair):
                if message is not None:
                    send_z(sign, *message)
        if k in after:
            after.pop(k)()
    shard(0)
    for k in sorted(after, reverse=True):
        after[k]()

    pull(fi, fo_r.at[0], sibling)
    kept, given = fo[core], fi[...]
    numer = jnp.where(core == 0, kept, given)
    pulled = jnp.where(core == 0, given, kept)
    lane = lax.broadcasted_iota(jnp.int32, (rows, width), 1)
    first = lax.broadcasted_iota(jnp.int32, (rows, width), 0) + (core * block + y * rows)

    def column(at):
        return jnp.sum(jnp.where(lane == first, line_of(at), 0.0), axis=1, keepdims=True)

    den = column(2 * x)
    inner = column(2 * x + 1) / den
    soft = numer / den
    q_out[...] = dot_nn(soft.astype(BF16), wu[...]).astype(BF16)
    grad_unit = (pulled - inner * numer) / den * logit_scale
    unit = own[0]
    grad_proj = (grad_unit - unit * jnp.sum(unit * grad_unit, axis=1, keepdims=True)) / own[1]
    gl_out[...] = dot_nt(grad_proj.astype(BF16), wd[...]).astype(BF16)

    for part in sorted(range(z_parts), key=lambda p: min(p, z_parts - 1 - p), reverse=True):
        at = pl.ds(part * z_rows, z_rows)
        c = cb[pl.ds(pl.multiple_of(tok * share + part * z_rows, z_rows), z_rows), :].astype(F32)
        cnorm = jnp.sqrt(jnp.sum(c * c, axis=1, keepdims=True) + epsilon)
        n = c / cnorm
        gn = ring_z.total(part, grad[0, at, :])
        gcb_out[at, :] = (gn - n * jnp.sum(n * gn, axis=1, keepdims=True)) / cnorm

    for copy in sent + ring_x.sent + ring_z.sent:
        copy.wait_send()


def place(*refs):
    n = len(refs) // 2
    copies = [pltpu.make_async_copy(refs[i], refs[n + i], refs[-1].at[i]) for i in range(n)]
    for copy in copies:
        copy.start()
    for copy in copies:
        copy.wait()


def solution(mesh):
    z_n = mesh.shape["tok"]
    x_n = X_CHIPS
    y_n = mesh.shape["code"] // (CORES * x_n)

    def local(latents, w_down, w_up, codebook, grad_out):
        rows, d = latents.shape
        lat_w = w_down.shape[1]
        codes = codebook.shape[0]
        width = CORES * y_n * rows
        sem = lambda *shape: pltpu.SemaphoreType.DMA(shape)
        ring = lambda n, parts, r, w: [
            pltpu.VMEM((2, n // 2, parts, r // parts, w), BF16),
            pltpu.VMEM((2, n // 2, parts, r // parts, w), BF16),
            sem(2, n // 2, parts),
            sem(2, n // 2, parts),
        ]
        any_space = pl.BlockSpec(memory_space=pl.ANY)
        vmem = pl.BlockSpec(memory_space=pltpu.VMEM)
        stats = (2 * x_n, width)
        outs = (
            jax.ShapeDtypeStruct((rows, d), BF16),
            jax.ShapeDtypeStruct((rows, d), BF16),
            jax.ShapeDtypeStruct((codes // z_n, lat_w), F32),
        )
        results = pl.pallas_call(
            functools.partial(kernel, x_n, y_n, z_n),
            out_shape=outs,
            in_specs=[any_space] * 5,
            out_specs=(vmem, vmem, vmem),
            scratch_shapes=[
                pltpu.VMEM(latents.shape, BF16),
                pltpu.VMEM(w_down.shape, BF16),
                pltpu.VMEM(w_up.shape, BF16),
                pltpu.VMEM(codebook.shape, BF16),
                pltpu.VMEM(grad_out.shape, BF16),
                sem(5),
                pltpu.VMEM((x_n, 2, width, lat_w), BF16),
                pltpu.VMEM((codes, lat_w), BF16),
                pltpu.VMEM((lat_w, codes), BF16),
                pltpu.VMEM((codes, 2 * x_n * width), BF16),
                pltpu.VMEM((lat_w, 2 * x_n * width), BF16),
                pltpu.VMEM((x_n, 2, lat_w, width), BF16),
                pltpu.VMEM((x_n, 2, lat_w, width), BF16),
                pltpu.VMEM((x_n, lat_w, width), BF16),
                pltpu.VMEM((z_n, codes // z_n, lat_w), F32),
                pltpu.VMEM((2, rows, lat_w), F32),
                sem(y_n - 1), sem(y_n - 1), sem(y_n, x_n - 1), sem(x_n - 1), sem(x_n), sem(x_n),
                pltpu.VMEM((3,) + stats, F32),
                pltpu.VMEM(stats, F32),
                pltpu.VMEM((y_n - 1,) + stats, F32),
                pltpu.VMEM((x_n - 1,) + stats, F32),
                sem(1), sem(1), sem(y_n - 1), sem(y_n - 1), sem(x_n - 1), sem(x_n - 1),
                sem(x_n), sem(x_n),
                *ring(x_n, 2, lat_w, width),
                pltpu.VMEM((y_n, CORES * rows, lat_w), BF16),
                pltpu.VMEM((y_n - 1, CORES * rows, lat_w), BF16),
                sem(y_n - 1), sem(y_n - 1),
                pltpu.VMEM((CORES, rows, lat_w), F32),
                pltpu.VMEM((rows, lat_w), F32),
                sem(1), sem(1),
                *ring(z_n, 4, codes // z_n, lat_w),
            ],
            compiler_params=pltpu.CompilerParams(
                collective_id=0, has_side_effects=True, vmem_limit_bytes=64 * 2**20 - 64 * 2**10
            ),
        )(latents, w_down, w_up, codebook, grad_out)
        return pl.pallas_call(
            place,
            out_shape=outs,
            in_specs=[vmem] * 3,
            out_specs=(any_space,) * 3,
            scratch_shapes=[sem(3)],
        )(*results)

    return jax.shard_map(
        local,
        mesh=mesh,
        in_specs=(P(("tok", "code"), None), P(), P(), P("code", None), P(("tok", "code"), None)),
        out_specs=(P(("tok", "code"), None), P(("tok", "code"), None), P(("code", "tok"), None)),
        check_vma=False,
    )
```

```python
import functools
import itertools

import jax
import jax.numpy as jnp
from jax import lax
from jax.experimental import pallas as pl
from jax.experimental.pallas import tpu as pltpu
from jax.sharding import PartitionSpec as P

MESH = pl.DeviceIdType.MESH
F32 = jnp.float32
BF16 = jnp.bfloat16

logit_scale = 64.0
epsilon = 1e-06
X_CHIPS = 4
CORES = 2


def dot_nn(a, b):
    return lax.dot_general(a, b, (((1,), (0,)), ((), ())), preferred_element_type=F32)


def dot_nt(a, b):
    return lax.dot_general(a, b, (((1,), (1,)), ((), ())), preferred_element_type=F32)


def longest(n, parts, sign, part):
    return n // 2 if (sign > 0) == (part < parts // 2) else n // 2 - 1


class RingSum:
    def __init__(self, n, out, into, send_sem, recv_sem, peer):
        self.n, self.out, self.into = n, out, into
        self.parts = out.shape[2]
        self.send_sem, self.recv_sem, self.peer = send_sem, recv_sem, peer
        self.sent = []

    def order(self, sign):
        listed = []
        for k in range(self.n // 2, 0, -1):
            parts = sorted(range(self.parts), key=lambda p: (longest(self.n, self.parts, sign, p), p))
            listed += [(k, p) for p in parts if k <= longest(self.n, self.parts, sign, p)]
        return listed

    def copy(self, sign, k, part):
        at = (0 if sign > 0 else 1, k - 1, part)
        return pltpu.make_async_remote_copy(
            src_ref=self.out.at[at],
            dst_ref=self.into.at[at],
            send_sem=self.send_sem.at[at],
            recv_sem=self.recv_sem.at[at],
            device_id=self.peer(sign),
            device_id_type=MESH,
        )

    def arrived(self, sign, k, part):
        self.copy(sign, k, part).wait_recv()
        return self.into[0 if sign > 0 else 1, k - 1, part].astype(F32)

    def send(self, sign, k, part, term):
        if k < longest(self.n, self.parts, sign, part):
            term = term + self.arrived(sign, k + 1, part)
        self.out[0 if sign > 0 else 1, k - 1, part] = term.astype(BF16)
        copy = self.copy(sign, k, part)
        copy.start()
        self.sent.append(copy)

    def total(self, part, term):
        for sign in (1, -1):
            if longest(self.n, self.parts, sign, part) >= 1:
                term = term + self.arrived(sign, 1, part)
        return term


def kernel(
    x_n, y_n, z_n,
    lat_h, wd_h, wu_h, cb_h, go_h,
    q_out, gl_out, gcb_out,
    lat, wd, wu, cb, go, load_sem, cb_s, cb_r,
    gat, low, low_t, ee, wt, tr, na, grad, own,
    ay_s, ay_r, ax_s, ax_r,
    st, st_y_in, st_x_in, sy_s, sy_r, sx_s, sx_r,
    xo, xi, xo_s, xo_r,
    yo, yi, yo_s, yo_r,
    co, ci, co_s, co_r,
    zo, zi, zo_s, zo_r,
):
    tok = lax.axis_index("tok")
    code = lax.axis_index("code")
    core = lax.rem(code, CORES)
    y = lax.rem(code // CORES, y_n)
    x = code // (CORES * y_n)
    rows = lat_h.shape[0]
    lat_w = wd_h.shape[1]
    codes = cb_h.shape[0]
    block = y_n * rows
    width = 2 * block
    z_parts = zo.shape[2]
    x_parts = xo.shape[2]
    share = codes // z_n
    z_rows = share // z_parts
    mine = core * codes
    other = (1 - core) * codes

    def at_code(x_at, y_at, core_at):
        return {"code": (x_at * y_n + y_at) * CORES + core_at}

    sibling = at_code(x, y, 1 - core)

    def y_peer(step):
        return at_code(x, lax.rem(y + step, y_n), core)

    def x_peer(step):
        return at_code(lax.rem(x + step + x_n, x_n), y, core)

    def z_peer(step):
        return {"tok": lax.rem(tok + step + z_n, z_n)}

    def remote(src, dst, send_sem, recv_sem, device):
        return pltpu.make_async_remote_copy(
            src_ref=src, dst_ref=dst, send_sem=send_sem, recv_sem=recv_sem, device_id=device, device_id_type=MESH
        )

    sent = []

    def push(*args):
        copy = remote(*args)
        copy.start()
        sent.append(copy)

    def drain():
        while sent:
            sent.pop(0).wait_send()

    def pull(dst, recv_sem, device):
        remote(dst, dst, cb_s.at[0], recv_sem, device).wait_recv()

    def span(start, size):
        return pl.ds(pl.multiple_of(start, size), size)

    loads = [
        pltpu.make_async_copy(src, dst, load_sem.at[i])
        for i, (src, dst) in enumerate(
            ((lat_h, lat), (wd_h, wd), (go_h, go), (wu_h, wu), (cb_h, cb.at[span(mine, codes), :]))
        )
    ]
    for load in loads:
        load.start()

    peers = [sibling] + [y_peer(s) for s in range(1, y_n)] + [x_peer(s) for s in range(1, x_n)]
    peers += [z_peer(1), z_peer(-1)]
    barrier = pltpu.get_barrier_semaphore()
    for peer in peers:
        pl.semaphore_signal(barrier, inc=1, device_id=peer, device_id_type=MESH)

    place_of = {j: i for i, j in enumerate((0, x_n - 1, 1, 2))}

    def chunk(j, start, size):
        pair, second = divmod(place_of[j], 2)
        return gat.at[pair, :, span(second * block + start, size), :]

    def lanes(j):
        return pl.ds(place_of[j] % 2 * block, block)

    loads[0].wait()
    loads[1].wait()
    proj = dot_nn(lat[...], wd[...])
    lnorm = jnp.sqrt(jnp.sum(proj * proj, axis=1, keepdims=True) + epsilon)
    unit = proj / lnorm
    own[0] = unit
    own[1] = jnp.broadcast_to(lnorm, unit.shape)
    gat[0, 0, span(y * rows, rows), :] = (unit.astype(BF16).astype(F32) * logit_scale).astype(BF16)
    loads[2].wait()
    loads[3].wait()
    gat[0, 1, span(y * rows, rows), :] = dot_nt(go[...], wu[...]).astype(BF16)

    pl.semaphore_wait(barrier, len(peers))

    near = sorted(range(1, y_n), key=lambda s: min(s, y_n - s))

    def along_x(s):
        from_y = lax.rem(y + y_n - s, y_n) * rows
        for i, step in enumerate((2, 1, -1)):
            slot = -step % x_n
            push(chunk(0, from_y, rows), chunk(slot, from_y, rows), ax_s.at[s, i], ax_r.at[slot - 1], x_peer(step))

    for s in near:
        piece = chunk(0, y * rows, rows)
        push(piece, piece, ay_s.at[s - 1], ay_r.at[s - 1], y_peer(s))
    along_x(0)
    push(cb_h, cb.at[span(mine, codes), :], cb_s.at[0], cb_r.at[0], sibling)

    step_rows = min(256, codes)
    steps = codes // step_rows

    def normalize(i):
        if i == 0:
            loads[4].wait()
        if i == steps:
            pull(cb.at[span(other, codes), :], cb_r.at[0], sibling)
        at = span((mine if i < steps else other) + i % steps * step_rows, step_rows)
        c = cb[at, :].astype(F32)
        n = c / jnp.sqrt(jnp.sum(c * c, axis=1, keepdims=True) + epsilon)
        n = n.astype(BF16)
        low[at, :] = n
        low_t[:, at] = n.T

    todo = list(range(2 * steps))
    for _ in range(min(6, steps)):
        normalize(todo.pop(0))
    for s in near:
        pull(chunk(0, lax.rem(y + y_n - s, y_n) * rows, rows), ay_r.at[s - 1], y_peer(s))
        along_x(s)
        if todo:
            normalize(todo.pop(0))
    for i in todo:
        normalize(i)

    tile = min(512, codes)
    sums = {}

    def forward(pair):
        u = gat[pair, 0]
        g = gat[pair, 1]
        col = pl.ds(pair * width, width)
        col_h = pl.ds((2 + pair) * width, width)

        def step(i, carry):
            den, inn = carry
            at = span(i * tile, tile)
            n = low[at, :]
            e = jnp.exp(dot_nt(n, u))
            eh = e * dot_nt(n, g)
            ee[at, col] = e.astype(BF16)
            ee[at, col_h] = eh.astype(BF16)
            return den + e.reshape(tile // 8, 8, width).sum(0), inn + eh.reshape(tile // 8, 8, width).sum(0)

        zero = jnp.zeros((8, width), F32)
        den, inn = lax.fori_loop(0, CORES * codes // tile, step, (zero, zero), unroll=True)
        sums[pair] = (jnp.sum(den, axis=0, keepdims=True), jnp.sum(inn, axis=0, keepdims=True))
        tr[pair, 0] = u.T
        tr[pair, 1] = g.T

    def weighted(pair):
        na[pair, 0] = dot_nn(low_t[...], ee[:, pl.ds(pair * width, width)]).astype(BF16)
        na[pair, 1] = dot_nn(low_t[...], ee[:, pl.ds((2 + pair) * width, width)]).astype(BF16)

    def from_x(j):
        pull(chunk(j, 0, block), ax_r.at[j - 1], x_peer(j))

    from_x(x_n - 1)
    forward(0)
    from_x(1)
    from_x(2)
    forward(1)

    line = lax.broadcasted_iota(jnp.int32, (2 * x_n, block), 0)
    part = jnp.zeros((2 * x_n, block), F32)
    for j in range(x_n):
        at_x = lax.rem(x + j, x_n)
        first = place_of[j] % 2 * block
        for i in range(2):
            part = jnp.where(line == 2 * at_x + i, sums[place_of[j] // 2][i][:, first : first + block], part)
    st[0] = part
    for s in reversed(near):
        push(st.at[0], st_y_in.at[s - 1], sy_s.at[s - 1], sy_r.at[s - 1], y_peer(s))
    weighted(0)
    weighted(1)
    drain()

    ring_x = RingSum(x_n, xo, xi, xo_s, xo_r, x_peer)

    def token_sum(j, kind):
        return na[place_of[j] // 2, kind, :, lanes(j)].astype(F32)

    def send_x(wanted):
        for sign in (1, -1):
            for k, kind in ring_x.order(sign):
                if wanted(k == longest(x_n, x_parts, sign, kind)):
                    ring_x.send(sign, k, kind, token_sum((sign * k) % x_n, kind))

    send_x(lambda begins: begins)

    for s in near:
        pull(st_y_in.at[s - 1], sy_r.at[s - 1], y_peer(s))
        part = part + st_y_in[s - 1]
    st[1] = part
    for s in range(1, x_n):
        push(st.at[1], st_x_in.at[s - 1], sx_s.at[s - 1], sx_r.at[s - 1], x_peer(s))
    send_x(lambda begins: not begins)
    for s in range(1, x_n):
        pull(st_x_in.at[s - 1], sx_r.at[s - 1], x_peer(s))
        part = part + st_x_in[s - 1]
    total = part

    def line_of(at):
        return jnp.sum(jnp.where(line == at, total, 0.0), axis=0, keepdims=True)

    for pair in range(2):
        at_x = [lax.rem(x + j, x_n) for j in sorted(place_of, key=place_of.get)[2 * pair : 2 * pair + 2]]
        den = jnp.concatenate([line_of(2 * at) for at in at_x], axis=1)
        inner = jnp.concatenate([line_of(2 * at + 1) for at in at_x], axis=1) / den
        inv = 1.0 / den
        ut = tr[pair, 0].astype(F32)
        gt = tr[pair, 1].astype(F32)
        wt[:, pl.ds(pair * width, width)] = ((gt - inner * ut) * inv).astype(BF16)
        wt[:, pl.ds((2 + pair) * width, width)] = (ut * inv).astype(BF16)

    ring_z = RingSum(z_n, zo, zi, zo_s, zo_r, z_peer)
    top = z_n // 2
    steps_z = [top]
    for k in range(top - 1, 0, -1):
        steps_z += [k, z_n - k]
    steps_z.append(0)

    def shard_rows(half, step):
        return span(half + lax.rem(tok + step, z_n) * share, share)

    def give(steps):
        for step in steps:
            co[step] = dot_nt(ee[shard_rows(other, step), :], wt[...]).astype(BF16)
        for step in steps:
            push(co.at[step], ci.at[step], co_s.at[step], co_r.at[step], sibling)

    def shards(steps):
        for step in steps:
            grad[step] = dot_nt(ee[shard_rows(mine, step), :], wt[...])
        for step in steps:
            pull(ci.at[step], co_r.at[step], sibling)
            grad[step] += ci[step].astype(F32)

    def send_z(sign, k, part):
        ring_z.send(sign, k, part, grad[(sign * k) % z_n, pl.ds(part * z_rows, z_rows), :])

    def tokens_y():
        for kind in range(2):
            both = ring_x.total(kind, token_sum(0, kind)).T.astype(BF16)
            yo[:, :, kind * lat_w : (kind + 1) * lat_w] = both.reshape(y_n, rows, lat_w)
        for s in range(1, y_n):
            push(yo.at[lax.rem(y + s, y_n)], yi.at[s - 1], yo_s.at[s - 1], yo_r.at[s - 1], y_peer(s))

    def send_all(wanted):
        order = [[m for m in ring_z.order(sign) if wanted(sign, *m)] for sign in (1, -1)]
        for pair in itertools.zip_longest(*order):
            for sign, message in zip((1, -1), pair):
                if message is not None:
                    send_z(sign, *message)

    def begins(sign, k, part):
        return k == longest(z_n, z_parts, sign, part)

    give(steps_z[:1])
    give(steps_z[1:3])
    shards(steps_z[:1])
    send_all(lambda sign, k, part: k == top and begins(sign, k, part))
    shards(steps_z[1:3])
    send_all(lambda sign, k, part: k < top and begins(sign, k, part))
    give(steps_z[3:])
    shards(steps_z[3:])
    for k in range(top - 1, 0, -1):
        send_all(lambda sign, at, part: at == k and not begins(sign, at, part))
        if k == top - 1:
            tokens_y()
    if top == 1:
        tokens_y()

    sums_own = yo[y].astype(F32)
    for s in near:
        pull(yi.at[s - 1], yo_r.at[s - 1], y_peer(s))
        sums_own = sums_own + yi[s - 1].astype(F32)
    numer = sums_own[:, :lat_w]
    pulled = sums_own[:, lat_w:]
    lane = lax.broadcasted_iota(jnp.int32, (rows, block), 1)
    first = lax.broadcasted_iota(jnp.int32, (rows, block), 0) + y * rows

    def column(at):
        return jnp.sum(jnp.where(lane == first, line_of(at), 0.0), axis=1, keepdims=True)

    den = column(2 * x)
    inner = column(2 * x + 1) / den
    soft = numer / den
    q_out[...] = dot_nn(soft.astype(BF16), wu[...]).astype(BF16)
    grad_unit = (pulled - inner * numer) / den * logit_scale
    unit = own[0]
    grad_proj = (grad_unit - unit * jnp.sum(unit * grad_unit, axis=1, keepdims=True)) / own[1]
    gl_out[...] = dot_nt(grad_proj.astype(BF16), wd[...]).astype(BF16)

    drain()
    ring_z.sent, last = ring_z.sent[-2 * z_parts :], ring_z.sent[: -2 * z_parts]
    for copy in ring_x.sent + last:
        copy.wait_send()

    for part in sorted(range(z_parts), key=lambda p: min(p, z_parts - 1 - p), reverse=True):
        at = pl.ds(part * z_rows, z_rows)
        c = cb[span(mine + tok * share + part * z_rows, z_rows), :].astype(F32)
        cnorm = jnp.sqrt(jnp.sum(c * c, axis=1, keepdims=True) + epsilon)
        n = c / cnorm
        gn = ring_z.total(part, grad[0, at, :])
        gcb_out[at, :] = (gn - n * jnp.sum(n * gn, axis=1, keepdims=True)) / cnorm

    for copy in ring_z.sent:
        copy.wait_send()


def place(*refs):
    n = len(refs) // 2
    copies = [pltpu.make_async_copy(refs[i], refs[n + i], refs[-1].at[i]) for i in range(n)]
    for copy in copies:
        copy.start()
    for copy in copies:
        copy.wait()


def solution(mesh):
    z_n = mesh.shape["tok"]
    x_n = X_CHIPS
    y_n = mesh.shape["code"] // (CORES * x_n)

    def local(latents, w_down, w_up, codebook, grad_out):
        rows, d = latents.shape
        lat_w = w_down.shape[1]
        codes = codebook.shape[0]
        width = 2 * y_n * rows
        sem = lambda *shape: pltpu.SemaphoreType.DMA(shape)
        ring = lambda n, parts, r, w: [
            pltpu.VMEM((2, n // 2, parts, r // parts, w), BF16),
            pltpu.VMEM((2, n // 2, parts, r // parts, w), BF16),
            sem(2, n // 2, parts),
            sem(2, n // 2, parts),
        ]
        any_space = pl.BlockSpec(memory_space=pl.ANY)
        vmem = pl.BlockSpec(memory_space=pltpu.VMEM)
        stats = (2 * x_n, width // 2)
        outs = (
            jax.ShapeDtypeStruct((rows, d), BF16),
            jax.ShapeDtypeStruct((rows, d), BF16),
            jax.ShapeDtypeStruct((codes // z_n, lat_w), F32),
        )
        results = pl.pallas_call(
            functools.partial(kernel, x_n, y_n, z_n),
            out_shape=outs,
            in_specs=[any_space] * 5,
            out_specs=(vmem, vmem, vmem),
            scratch_shapes=[
                pltpu.VMEM(latents.shape, BF16),
                pltpu.VMEM(w_down.shape, BF16),
                pltpu.VMEM(w_up.shape, BF16),
                pltpu.VMEM((CORES * codes, lat_w), BF16),
                pltpu.VMEM(grad_out.shape, BF16),
                sem(5), sem(1), sem(1),
                pltpu.VMEM((2, 2, width, lat_w), BF16),
                pltpu.VMEM((CORES * codes, lat_w), BF16),
                pltpu.VMEM((lat_w, CORES * codes), BF16),
                pltpu.VMEM((CORES * codes, 4 * width), BF16),
                pltpu.VMEM((lat_w, 4 * width), BF16),
                pltpu.VMEM((2, 2, lat_w, width), BF16),
                pltpu.VMEM((2, 2, lat_w, width), BF16),
                pltpu.VMEM((z_n, codes // z_n, lat_w), F32),
                pltpu.VMEM((2, rows, lat_w), F32),
                sem(y_n - 1), sem(y_n - 1), sem(y_n, x_n - 1), sem(x_n - 1),
                pltpu.VMEM((2,) + stats, F32),
                pltpu.VMEM((y_n - 1,) + stats, F32),
                pltpu.VMEM((x_n - 1,) + stats, F32),
                sem(y_n - 1), sem(y_n - 1), sem(x_n - 1), sem(x_n - 1),
                *ring(x_n, 2, 2 * lat_w, width // 2),
                pltpu.VMEM((y_n, rows, 2 * lat_w), BF16),
                pltpu.VMEM((y_n - 1, rows, 2 * lat_w), BF16),
                sem(y_n - 1), sem(y_n - 1),
                pltpu.VMEM((z_n, codes // z_n, lat_w), BF16),
                pltpu.VMEM((z_n, codes // z_n, lat_w), BF16),
                sem(z_n), sem(z_n),
                *ring(z_n, 4, codes // z_n, lat_w),
            ],
            compiler_params=pltpu.CompilerParams(
                collective_id=0, has_side_effects=True, vmem_limit_bytes=64 * 2**20 - 64 * 2**10
            ),
        )(latents, w_down, w_up, codebook, grad_out)
        return pl.pallas_call(
            place,
            out_shape=outs,
            in_specs=[vmem] * 3,
            out_specs=(any_space,) * 3,
            scratch_shapes=[sem(3)],
        )(*results)

    return jax.shard_map(
        local,
        mesh=mesh,
        in_specs=(P(("tok", "code"), None), P(), P(), P("code", None), P(("tok", "code"), None)),
        out_specs=(P(("tok", "code"), None), P(("tok", "code"), None), P(("code", "tok"), None)),
        check_vma=False,
    )
```

```python
import functools
import itertools

import jax
import jax.numpy as jnp
from jax import lax
from jax.experimental import pallas as pl
from jax.experimental.pallas import tpu as pltpu
from jax.sharding import PartitionSpec as P

MESH = pl.DeviceIdType.MESH
F32 = jnp.float32
BF16 = jnp.bfloat16

logit_scale = 64.0
epsilon = 1e-06
X_CHIPS = 4
CORES = 2


def dot_nn(a, b):
    return lax.dot_general(a, b, (((1,), (0,)), ((), ())), preferred_element_type=F32)


def dot_nt(a, b):
    return lax.dot_general(a, b, (((1,), (1,)), ((), ())), preferred_element_type=F32)


def longest(n, parts, sign, part):
    return n // 2 if (sign > 0) == (part < parts // 2) else n // 2 - 1


class RingSum:
    def __init__(self, n, out, into, send_sem, recv_sem, peer):
        self.n, self.out, self.into = n, out, into
        self.parts = out.shape[2]
        self.send_sem, self.recv_sem, self.peer = send_sem, recv_sem, peer
        self.sent = []

    def order(self, sign):
        listed = []
        for k in range(self.n // 2, 0, -1):
            parts = sorted(range(self.parts), key=lambda p: (longest(self.n, self.parts, sign, p), p))
            listed += [(k, p) for p in parts if k <= longest(self.n, self.parts, sign, p)]
        return listed

    def copy(self, sign, k, part):
        at = (0 if sign > 0 else 1, k - 1, part)
        return pltpu.make_async_remote_copy(
            src_ref=self.out.at[at],
            dst_ref=self.into.at[at],
            send_sem=self.send_sem.at[at],
            recv_sem=self.recv_sem.at[at],
            device_id=self.peer(sign),
            device_id_type=MESH,
        )

    def arrived(self, sign, k, part):
        self.copy(sign, k, part).wait_recv()
        return self.into[0 if sign > 0 else 1, k - 1, part].astype(F32)

    def send(self, sign, k, part, term):
        if k < longest(self.n, self.parts, sign, part):
            term = term + self.arrived(sign, k + 1, part)
        self.out[0 if sign > 0 else 1, k - 1, part] = term.astype(BF16)
        copy = self.copy(sign, k, part)
        copy.start()
        self.sent.append(copy)

    def total(self, part, term):
        for sign in (1, -1):
            if longest(self.n, self.parts, sign, part) >= 1:
                term = term + self.arrived(sign, 1, part)
        return term


def kernel(
    x_n, y_n, z_n,
    lat_h, wd_h, wu_h, cb_h, go_h,
    q_hbm, gl_hbm, gcb_hbm,
    lat, wd, wu, cb, go, load_sem, cb_s, cb_r,
    gat, low, low_t, ee, wt, tr, na, grad, own,
    ay_s, ay_r, ax_s, ax_r,
    st, st_y_in, st_x_in, sy_s, sy_r, sx_s, sx_r,
    xo, xi, xo_s, xo_r,
    yo, yi, yo_s, yo_r,
    co, ci, co_s, co_r,
    zo, zi, zo_s, zo_r,
    q_out, gl_out, gcb_out, fin, out_sem,
):
    tok = lax.axis_index("tok")
    code = lax.axis_index("code")
    core = lax.rem(code, CORES)
    y = lax.rem(code // CORES, y_n)
    x = code // (CORES * y_n)
    rows = lat_h.shape[0]
    lat_w = wd_h.shape[1]
    codes = cb_h.shape[0]
    block = y_n * rows
    width = 2 * block
    z_parts = zo.shape[2]
    x_parts = xo.shape[2]
    share = codes // z_n
    z_rows = share // z_parts
    mine = core * codes
    other = (1 - core) * codes

    def at_code(x_at, y_at, core_at):
        return {"code": (x_at * y_n + y_at) * CORES + core_at}

    sibling = at_code(x, y, 1 - core)

    def y_peer(step):
        return at_code(x, lax.rem(y + step, y_n), core)

    def x_peer(step):
        return at_code(lax.rem(x + step + x_n, x_n), y, core)

    def z_peer(step):
        return {"tok": lax.rem(tok + step + z_n, z_n)}

    def remote(src, dst, send_sem, recv_sem, device):
        return pltpu.make_async_remote_copy(
            src_ref=src, dst_ref=dst, send_sem=send_sem, recv_sem=recv_sem, device_id=device, device_id_type=MESH
        )

    sent = []

    def push(*args):
        copy = remote(*args)
        copy.start()
        sent.append(copy)

    def drain():
        while sent:
            sent.pop(0).wait_send()

    def pull(dst, recv_sem, device):
        remote(dst, dst, cb_s.at[0], recv_sem, device).wait_recv()

    def span(start, size):
        return pl.ds(pl.multiple_of(start, size), size)

    peers = [sibling] + [y_peer(s) for s in range(1, y_n)] + [x_peer(s) for s in range(1, x_n)]
    peers += [z_peer(1), z_peer(-1)]
    barrier = pltpu.get_barrier_semaphore()
    for peer in peers:
        pl.semaphore_signal(barrier, inc=1, device_id=peer, device_id_type=MESH)

    loads = [
        pltpu.make_async_copy(src, dst, load_sem.at[i])
        for i, (src, dst) in enumerate(
            ((lat_h, lat), (wd_h, wd), (go_h, go), (wu_h, wu), (cb_h, cb.at[span(mine, codes), :]))
        )
    ]
    for load in loads:
        load.start()

    def chunk(j, start, size):
        return gat.at[j, :, span(start, size), :]

    loads[0].wait()
    loads[1].wait()
    proj = dot_nn(lat[...], wd[...])
    lnorm = jnp.sqrt(jnp.sum(proj * proj, axis=1, keepdims=True) + epsilon)
    unit = proj / lnorm
    own[0] = unit
    own[1] = jnp.broadcast_to(lnorm, unit.shape)
    gat[0, 0, span(y * rows, rows), :] = (unit.astype(BF16).astype(F32) * logit_scale).astype(BF16)
    loads[2].wait()
    loads[3].wait()
    gat[0, 1, span(y * rows, rows), :] = dot_nt(go[...], wu[...]).astype(BF16)

    pl.semaphore_wait(barrier, len(peers))

    near = sorted(range(1, y_n), key=lambda s: min(s, y_n - s))

    def along_x(s):
        from_y = lax.rem(y + y_n - s, y_n) * rows
        for i, step in enumerate((2, 1, -1)):
            slot = -step % x_n
            push(chunk(0, from_y, rows), chunk(slot, from_y, rows), ax_s.at[s, i], ax_r.at[slot - 1], x_peer(step))

    for s in near:
        piece = chunk(0, y * rows, rows)
        push(piece, piece, ay_s.at[s - 1], ay_r.at[s - 1], y_peer(s))
    along_x(0)
    push(cb_h, cb.at[span(mine, codes), :], cb_s.at[0], cb_r.at[0], sibling)

    step_rows = min(256, codes)
    steps = codes // step_rows

    def normalize(i):
        if i == 0:
            loads[4].wait()
        if i == steps:
            pull(cb.at[span(other, codes), :], cb_r.at[0], sibling)
        at = span((mine if i < steps else other) + i % steps * step_rows, step_rows)
        c = cb[at, :].astype(F32)
        n = c / jnp.sqrt(jnp.sum(c * c, axis=1, keepdims=True) + epsilon)
        n = n.astype(BF16)
        low[at, :] = n
        low_t[:, at] = n.T

    todo = list(range(2 * steps))
    for _ in range(min(6, steps)):
        normalize(todo.pop(0))
    for s in near:
        pull(chunk(0, lax.rem(y + y_n - s, y_n) * rows, rows), ay_r.at[s - 1], y_peer(s))
        along_x(s)
        if todo:
            normalize(todo.pop(0))
    for i in todo:
        normalize(i)

    tile = min(512, codes)
    sums = {}

    def forward(j):
        both = gat[j].reshape(width, lat_w)
        col = pl.ds(j * width, block)
        col_h = pl.ds(j * width + block, block)

        def step(i, carry):
            den, inn = carry
            at = span(i * tile, tile)
            products = dot_nt(low[at, :], both)
            e = jnp.exp(products[:, :block])
            eh = e * products[:, block:]
            ee[at, col] = e.astype(BF16)
            ee[at, col_h] = eh.astype(BF16)
            return den + e.reshape(tile // 8, 8, block).sum(0), inn + eh.reshape(tile // 8, 8, block).sum(0)

        zero = jnp.zeros((8, block), F32)
        den, inn = lax.fori_loop(0, CORES * codes // tile, step, (zero, zero), unroll=True)
        sums[j] = (jnp.sum(den, axis=0, keepdims=True), jnp.sum(inn, axis=0, keepdims=True))
        tr[j] = both.T

    def weighted(j):
        na[j] = dot_nn(low_t[...], ee[:, pl.ds(j * width, width)]).astype(BF16)

    def from_x(j):
        pull(chunk(j, 0, block), ax_r.at[j - 1], x_peer(j))

    forward(0)
    arriving = (x_n - 1, 1, 2)
    for j in arriving:
        from_x(j)
        forward(j)

    line = lax.broadcasted_iota(jnp.int32, (2 * x_n, block), 0)
    part = jnp.zeros((2 * x_n, block), F32)
    for j in range(x_n):
        at_x = lax.rem(x + j, x_n)
        for i in range(2):
            part = jnp.where(line == 2 * at_x + i, sums[j][i], part)
    st[0] = part
    for s in reversed(near):
        push(st.at[0], st_y_in.at[s - 1], sy_s.at[s - 1], sy_r.at[s - 1], y_peer(s))
    for j in (0,) + arriving:
        weighted(j)
    drain()

    ring_x = RingSum(x_n, xo, xi, xo_s, xo_r, x_peer)

    def token_sum(j, kind):
        return na[j, :, pl.ds(kind * block, block)].astype(F32)

    def send_x(wanted):
        for sign in (1, -1):
            for k, kind in ring_x.order(sign):
                if wanted(k == longest(x_n, x_parts, sign, kind)):
                    ring_x.send(sign, k, kind, token_sum((sign * k) % x_n, kind))

    send_x(lambda begins: begins)

    for s in near:
        pull(st_y_in.at[s - 1], sy_r.at[s - 1], y_peer(s))
        part = part + st_y_in[s - 1]
    st[1] = part
    for s in range(1, x_n):
        push(st.at[1], st_x_in.at[s - 1], sx_s.at[s - 1], sx_r.at[s - 1], x_peer(s))
    send_x(lambda begins: not begins)
    for s in range(1, x_n):
        pull(st_x_in.at[s - 1], sx_r.at[s - 1], x_peer(s))
        part = part + st_x_in[s - 1]
    total = part

    def line_of(at):
        return jnp.sum(jnp.where(line == at, total, 0.0), axis=0, keepdims=True)

    for j in range(x_n):
        at_x = lax.rem(x + j, x_n)
        den = line_of(2 * at_x)
        inner = line_of(2 * at_x + 1) / den
        inv = 1.0 / den
        ut = tr[j, :, :block].astype(F32)
        gt = tr[j, :, block:].astype(F32)
        wt[:, pl.ds(j * width, block)] = ((gt - inner * ut) * inv).astype(BF16)
        wt[:, pl.ds(j * width + block, block)] = (ut * inv).astype(BF16)

    ring_z = RingSum(z_n, zo, zi, zo_s, zo_r, z_peer)
    top = z_n // 2
    steps_z = [top]
    for k in range(top - 1, 0, -1):
        steps_z += [k, z_n - k]
    steps_z.append(0)

    def shard_rows(half, step):
        return span(half + lax.rem(tok + step, z_n) * share, share)

    def give(steps):
        for step in steps:
            co[step] = dot_nt(ee[shard_rows(other, step), :], wt[...]).astype(BF16)
        for step in steps:
            push(co.at[step], ci.at[step], co_s.at[step], co_r.at[step], sibling)

    def shards(steps):
        for step in steps:
            grad[step] = dot_nt(ee[shard_rows(mine, step), :], wt[...])
        for step in steps:
            pull(ci.at[step], co_r.at[step], sibling)
            grad[step] += ci[step].astype(F32)

    def send_z(sign, k, part):
        ring_z.send(sign, k, part, grad[(sign * k) % z_n, pl.ds(part * z_rows, z_rows), :])

    def tokens_y():
        for kind in range(2):
            both = ring_x.total(kind, token_sum(0, kind)).T.astype(BF16)
            yo[:, :, kind * lat_w : (kind + 1) * lat_w] = both.reshape(y_n, rows, lat_w)
        for s in range(1, y_n):
            push(yo.at[lax.rem(y + s, y_n)], yi.at[s - 1], yo_s.at[s - 1], yo_r.at[s - 1], y_peer(s))

    def send_all(wanted):
        order = [[m for m in ring_z.order(sign) if wanted(sign, *m)] for sign in (1, -1)]
        for pair in itertools.zip_longest(*order):
            for sign, message in zip((1, -1), pair):
                if message is not None:
                    send_z(sign, *message)

    def begins(sign, k, part):
        return k == longest(z_n, z_parts, sign, part)

    give(steps_z[:1])
    give(steps_z[1:3])
    shards(steps_z[:1])
    send_all(lambda sign, k, part: k == top and begins(sign, k, part))
    shards(steps_z[1:3])
    send_all(lambda sign, k, part: k < top and begins(sign, k, part))
    give(steps_z[3:])
    shards(steps_z[3:5])
    tokens_y()
    for k in range(top - 1, 0, -1):
        for top_at in (top - 1, top):
            send_all(
                lambda sign, at, part: at == k
                and longest(z_n, z_parts, sign, part) == top_at
                and not begins(sign, at, part)
            )
            if k == top - 2 and top_at == top - 1:
                shards(steps_z[5:])
    if top < 3:
        shards(steps_z[5:])

    sums_own = yo[y].astype(F32)
    for s in near:
        pull(yi.at[s - 1], yo_r.at[s - 1], y_peer(s))
        sums_own = sums_own + yi[s - 1].astype(F32)
    numer = sums_own[:, :lat_w]
    pulled = sums_own[:, lat_w:]
    lane = lax.broadcasted_iota(jnp.int32, (rows, block), 1)
    first = lax.broadcasted_iota(jnp.int32, (rows, block), 0) + y * rows

    def column(at):
        return jnp.sum(jnp.where(lane == first, line_of(at), 0.0), axis=1, keepdims=True)

    den = column(2 * x)
    inner = column(2 * x + 1) / den
    soft = numer / den
    q_out[...] = dot_nn(soft.astype(BF16), wu[...]).astype(BF16)
    grad_unit = (pulled - inner * numer) / den * logit_scale
    unit = own[0]
    grad_proj = (grad_unit - unit * jnp.sum(unit * grad_unit, axis=1, keepdims=True)) / own[1]
    gl_out[...] = dot_nt(grad_proj.astype(BF16), wd[...]).astype(BF16)
    outs = [
        pltpu.make_async_copy(q_out, q_hbm, out_sem.at[0]),
        pltpu.make_async_copy(gl_out, gl_hbm, out_sem.at[1]),
    ]
    for copy in outs:
        copy.start()

    drain()
    ring_z.sent, last = ring_z.sent[-2 * z_parts :], ring_z.sent[: -2 * z_parts]
    for copy in ring_x.sent + last:
        copy.wait_send()

    c = cb[span(mine + tok * share, share), :].astype(F32)
    inv = 1.0 / jnp.sqrt(jnp.sum(c * c, axis=1, keepdims=True) + epsilon)
    fin[0] = c * inv
    fin[1] = jnp.broadcast_to(inv, c.shape)
    for part in sorted(range(z_parts), key=lambda p: (p % (z_parts // 2), p)):
        at = pl.ds(part * z_rows, z_rows)
        n = fin[0, at, :]
        gn = ring_z.total(part, grad[0, at, :])
        gcb_out[at, :] = (gn - n * jnp.sum(n * gn, axis=1, keepdims=True)) * fin[1, at, :]
        copy = pltpu.make_async_copy(gcb_out.at[at, :], gcb_hbm.at[at, :], out_sem.at[2 + part])
        copy.start()
        outs.append(copy)

    for copy in outs:
        copy.wait()
    for copy in ring_z.sent:
        copy.wait_send()


def place(*refs):
    n = len(refs) // 2
    copies = [pltpu.make_async_copy(refs[i], refs[n + i], refs[-1].at[i]) for i in range(n)]
    for copy in copies:
        copy.start()
    for copy in copies:
        copy.wait()


def solution(mesh):
    z_n = mesh.shape["tok"]
    x_n = X_CHIPS
    y_n = mesh.shape["code"] // (CORES * x_n)

    def local(latents, w_down, w_up, codebook, grad_out):
        rows, d = latents.shape
        lat_w = w_down.shape[1]
        codes = codebook.shape[0]
        width = 2 * y_n * rows
        sem = lambda *shape: pltpu.SemaphoreType.DMA(shape)
        ring = lambda n, parts, r, w: [
            pltpu.VMEM((2, n // 2, parts, r // parts, w), BF16),
            pltpu.VMEM((2, n // 2, parts, r // parts, w), BF16),
            sem(2, n // 2, parts),
            sem(2, n // 2, parts),
        ]
        any_space = pl.BlockSpec(memory_space=pl.ANY)
        vmem = pl.BlockSpec(memory_space=pltpu.VMEM)
        stats = (2 * x_n, width // 2)
        outs = (
            jax.ShapeDtypeStruct((rows, d), BF16),
            jax.ShapeDtypeStruct((rows, d), BF16),
            jax.ShapeDtypeStruct((codes // z_n, lat_w), F32),
        )
        results = pl.pallas_call(
            functools.partial(kernel, x_n, y_n, z_n),
            out_shape=outs,
            in_specs=[any_space] * 5,
            out_specs=(any_space,) * 3,
            scratch_shapes=[
                pltpu.VMEM(latents.shape, BF16),
                pltpu.VMEM(w_down.shape, BF16),
                pltpu.VMEM(w_up.shape, BF16),
                pltpu.VMEM((CORES * codes, lat_w), BF16),
                pltpu.VMEM(grad_out.shape, BF16),
                sem(5), sem(1), sem(1),
                pltpu.VMEM((x_n, 2, width // 2, lat_w), BF16),
                pltpu.VMEM((CORES * codes, lat_w), BF16),
                pltpu.VMEM((lat_w, CORES * codes), BF16),
                pltpu.VMEM((CORES * codes, x_n * width), BF16),
                pltpu.VMEM((lat_w, x_n * width), BF16),
                pltpu.VMEM((x_n, lat_w, width), BF16),
                pltpu.VMEM((x_n, lat_w, width), BF16),
                pltpu.VMEM((z_n, codes // z_n, lat_w), F32),
                pltpu.VMEM((2, rows, lat_w), F32),
                sem(y_n - 1), sem(y_n - 1), sem(y_n, x_n - 1), sem(x_n - 1),
                pltpu.VMEM((2,) + stats, F32),
                pltpu.VMEM((y_n - 1,) + stats, F32),
                pltpu.VMEM((x_n - 1,) + stats, F32),
                sem(y_n - 1), sem(y_n - 1), sem(x_n - 1), sem(x_n - 1),
                *ring(x_n, 2, 2 * lat_w, width // 2),
                pltpu.VMEM((y_n, rows, 2 * lat_w), BF16),
                pltpu.VMEM((y_n - 1, rows, 2 * lat_w), BF16),
                sem(y_n - 1), sem(y_n - 1),
                pltpu.VMEM((z_n, codes // z_n, lat_w), BF16),
                pltpu.VMEM((z_n, codes // z_n, lat_w), BF16),
                sem(z_n), sem(z_n),
                *ring(z_n, 4, codes // z_n, lat_w),
                pltpu.VMEM((rows, d), BF16),
                pltpu.VMEM((rows, d), BF16),
                pltpu.VMEM((codes // z_n, lat_w), F32),
                pltpu.VMEM((2, codes // z_n, lat_w), F32),
                sem(2 + 4),
            ],
            compiler_params=pltpu.CompilerParams(
                collective_id=0, has_side_effects=True, vmem_limit_bytes=64 * 2**20 - 64 * 2**10
            ),
        )(latents, w_down, w_up, codebook, grad_out)
        return pl.pallas_call(
            place,
            out_shape=outs,
            in_specs=[vmem] * 3,
            out_specs=(any_space,) * 3,
            scratch_shapes=[sem(3)],
        )(*results)

    return jax.shard_map(
        local,
        mesh=mesh,
        in_specs=(P(("tok", "code"), None), P(), P(), P("code", None), P(("tok", "code"), None)),
        out_specs=(P(("tok", "code"), None), P(("tok", "code"), None), P(("code", "tok"), None)),
        check_vma=False,
    )
```
